128 devices in a mesh: dp: 8 (over z_lo, y), section: 16 (over z_hi, x, core).
Axes of the slice: x: 4, y: 4, z: 4 (z_hi: 2, z_lo: 2; z = z_hi * 2 + z_lo), core: 2. Of those that a mesh axis runs over, the one named last changes fastest.
Arguments:
- layer_in: bfloat16 [16, 16, 64, 6144], P('section', None, 'dp'), may hold values from -6 to 6
- pre_act: bfloat16 [16, 16, 64, 6144], P('section', None, 'dp'), may hold values from -8 to 8
- weight: bfloat16 [16, 6144, 6144], P('section', 'dp'), may hold values from -1 to 1
- gain: float32 [16, 6144], P('section'), may hold values from 0.5 to 1.5
- cot_top: bfloat16 [16, 64, 6144], P(None, 'dp', 'section'), may hold values from -6 to 6
Outputs:
- cot_bottom: bfloat16 [16, 64, 6144], P(None, 'dp', 'section')
- weight_grad: bfloat16 [16, 6144, 6144], P('section', 'dp')
- gain_grad: float32 [16, 6144], P('section', 'dp')
The draws below stay inside these ranges and needn't reach their ends.
All inputs are finite; a program needn't handle non-finite values.
Results may differ from the reference program's by a relative error of at most 0.035.
Values may be sent and summed in bfloat16 or wider, within the bound.
No kernel may reach another device: no remote copies, remote signals or barrier semaphores. Data moves between devices by JAX's collectives and lax.ppermute only.
A program may use at most 192 MiB of HBM per device.

```python
import jax
import jax.numpy as jnp
from jax import lax

D = 6144
MICRO = 16
TOKENS = 64
LAYERS = 16


def shared_base(key):
    return jnp.clip(jax.random.normal(key, (MICRO, TOKENS, D), jnp.float32), -4.0, 4.0)


def draw_layer_in(key, part):
    base = shared_base(key)
    key = jax.random.fold_in(key, 11)
    noise = jnp.clip(jax.random.normal(key, (LAYERS, MICRO, TOKENS, D), jnp.float32), -4.0, 4.0)
    mixed = 0.6 * base[None] + 0.8 * noise
    return mixed.astype(jnp.bfloat16)


def draw_cot_top(key, part):
    base = shared_base(key)
    key = jax.random.fold_in(key, 13)
    noise = jnp.clip(jax.random.normal(key, (MICRO, TOKENS, D), jnp.float32), -4.0, 4.0)
    mixed = 0.6 * base + 0.8 * noise
    return mixed.astype(jnp.bfloat16)


def draw_weight(key, part):
    key = jax.random.fold_in(key, 17)
    noise = jnp.clip(jax.random.normal(key, (LAYERS, D, D), jnp.float32), -6.0, 6.0)
    diagonal = (lax.broadcasted_iota(jnp.int32, (D, D), 0) == lax.broadcasted_iota(jnp.int32, (D, D), 1)).astype(jnp.float32)
    mixed = noise / jnp.sqrt(jnp.float32(D)) - 0.5 * diagonal[None]
    return mixed.astype(jnp.bfloat16)


def block_levels(stream_key, dims, shards, low, top_value):
    level, own = 1.0, jax.random.fold_in(stream_key, 6)
    for axis_at, parts in shards:
        steps = jnp.exp(jax.random.uniform(jax.random.fold_in(own, axis_at), (parts,), jnp.float32, low / len(shards), top_value / len(shards)))
        level = level * jnp.repeat(steps, dims[axis_at] // parts).reshape([-1 if axis == axis_at else 1 for axis in range(len(dims))])
    return level


def bell_draw(key, dims, scale, reach, pieces=(), held_as=jnp.bfloat16):
    factor_of = block_levels(key, dims, pieces, -0.22, 0.18) if pieces else 1.0
    drawn = jax.random.normal(key, dims, jnp.float32) * scale * factor_of
    return jnp.minimum(jnp.maximum(drawn, -reach), reach).astype(held_as)


def setup_inputs(seed: int = 0) -> dict:
    seeds = jax.random.split(jax.random.key(seed), 6)
    return {
        "layer_in": draw_layer_in(jax.random.fold_in(seeds[5], 71), 0),
        "pre_act": bell_draw(seeds[1], (LAYERS, MICRO, TOKENS, D), 1.5, 8.0, ((0, 16), (2, 8))),
        "weight": draw_weight(jax.random.fold_in(seeds[5], 71), 0),
        "gain": jnp.clip(1.0 + 0.1 * jax.random.normal(seeds[3], (LAYERS, D), jnp.float32), 0.5, 1.5),
        "cot_top": draw_cot_top(jax.random.fold_in(seeds[5], 71), 0),
    }


norm_eps = 1e-05

def layer_back(incoming, inputs, pre_acts, weight_rows, gain_row):
    model_width = inputs.shape[-1]
    inputs_f = inputs.astype(jnp.float32)
    row_scale = lax.rsqrt(lax.optimization_barrier(jnp.mean(inputs_f * inputs_f, axis=-1, keepdims=True)) + norm_eps)
    normed = (inputs_f * row_scale * gain_row).astype(jnp.bfloat16)
    pre_f = pre_acts.astype(jnp.float32)
    sigmoid_z = jax.nn.sigmoid(pre_f)
    slope_all = sigmoid_z * (1.0 + pre_f * (1.0 - sigmoid_z))
    pre_grad = (incoming.astype(jnp.float32) * slope_all).astype(jnp.bfloat16)
    flat_grad = pre_grad.reshape(-1, model_width)
    norm_grad = jnp.dot(flat_grad, weight_rows.T, preferred_element_type=jnp.float32).reshape(inputs.shape)
    scaled = gain_row * norm_grad
    row_dot = lax.optimization_barrier(jnp.sum(scaled * inputs_f, axis=-1, keepdims=True))
    cubed = row_scale * row_scale * row_scale
    out_grad = (incoming.astype(jnp.float32) + row_scale * scaled - inputs_f * cubed * row_dot / model_width).astype(jnp.bfloat16)
    gain_grad = lax.optimization_barrier(jnp.sum(norm_grad * inputs_f * row_scale, axis=(0, 1)))
    weight_grad = jnp.dot(normed.reshape(-1, model_width).T, flat_grad, preferred_element_type=jnp.float32).astype(jnp.bfloat16)
    return (out_grad, weight_grad, gain_grad)

def reference(layer_in, pre_act, weight, gain, cot_top):

    def layer_step(incoming, layer_args):
        inputs, pre_acts, weight_rows, gain_row = layer_args
        out_grad, weight_grad, gain_grad = layer_back(incoming, inputs, pre_acts, weight_rows, gain_row)
        return (out_grad, (weight_grad, gain_grad))
    bottom, grads = lax.scan(layer_step, cot_top, (layer_in, pre_act, weight, gain), reverse=True)
    return (bottom, grads[0], grads[1])
```

```python
import jax
import jax.numpy as jnp
from jax import lax
from jax.experimental import pallas as pl
from jax.experimental.pallas import tpu as pltpu
from jax.sharding import PartitionSpec as P

norm_eps = 1e-05
LANES = 128
EXTRA = 16


def pass_down(value):
    count = lax.axis_size("section")
    return lax.ppermute(value, "section", [(source, source - 1) for source in range(1, count)])


def spread(value):
    count = lax.axis_size("dp")
    copies = jnp.broadcast_to(value[None], (count,) + value.shape)
    return lax.all_to_all(copies, "dp", split_axis=0, concat_axis=0, tiled=True)


def slope_of(pre_acts):
    pre_f = pre_acts.astype(jnp.float32)
    sigmoid_z = jax.nn.sigmoid(pre_f)
    return sigmoid_z * (1.0 + pre_f * (1.0 - sigmoid_z))


def split3(value):
    high = value.astype(jnp.bfloat16)
    rest = value - high.astype(jnp.float32)
    mid = rest.astype(jnp.bfloat16)
    low = (rest - mid.astype(jnp.float32)).astype(jnp.bfloat16)
    return jnp.stack([high, mid, low])


def tick_kernel(tokens, parts, width):
    cols = width // parts
    pieces = cols // LANES
    body_rows = pieces * tokens
    rows = body_rows + EXTRA
    across = (((1,), (1,)), ((), ()))
    down = (((0,), (0,)), ((), ()))

    def body(live, gathered, upper, weight_t, part, x_upper, x_own, scale, gain, acc_in, part_out, pre_out, acc_out):
        sums = jnp.concatenate([gathered[d, body_rows:rows, :] for d in range(parts)], axis=0)
        coef = lax.dot_general(
            sums, jnp.ones((parts * EXTRA, LANES), jnp.bfloat16), down, preferred_element_type=jnp.float32
        )[:tokens]
        for d in range(parts):
            for j in range(pieces):
                at = (d * pieces + j) * LANES
                piece = gathered[d, j * tokens : (j + 1) * tokens, :].astype(jnp.float32)
                piece = piece - coef * upper[:, at : at + LANES].astype(jnp.float32)
                pre_out[:, at : at + LANES] = piece.astype(jnp.bfloat16)
        norm_grad = jnp.dot(pre_out[...], weight_t[...], preferred_element_type=jnp.float32)
        scale_v = scale[...]
        total = jnp.zeros((tokens, LANES), jnp.float32)
        for j in range(pieces):
            here = slice(j * tokens, (j + 1) * tokens)
            lanes = slice(j * LANES, (j + 1) * LANES)
            grad_j = norm_grad[:, lanes]
            x_j = x_own[here, :].astype(jnp.float32)
            scaled = gain[:, lanes] * grad_j
            incoming = part[here, :].astype(jnp.float32) - coef * x_upper[here, :].astype(jnp.float32)
            part_out[here, :] = (incoming + scale_v * scaled).astype(jnp.bfloat16)
            total = total + scaled * x_j
            gain_sum = jnp.sum(grad_j * x_j * scale_v, axis=0, keepdims=True)
            acc_out[:, lanes] = acc_in[:, lanes] + jnp.where(live[0] > 0, gain_sum, 0.0)
        total = total * (scale_v * scale_v * scale_v * (1.0 / width))
        if tokens < LANES:
            total = jnp.concatenate([total, jnp.zeros((LANES - tokens, LANES), jnp.float32)], axis=0)
        high = total.astype(jnp.bfloat16)
        low = (total - high.astype(jnp.float32)).astype(jnp.bfloat16)
        ones = jnp.ones((EXTRA, LANES), jnp.bfloat16)
        line = lax.dot_general(ones, high, across, preferred_element_type=jnp.float32)
        line = line + lax.dot_general(ones, low, across, preferred_element_type=jnp.float32)
        line_high = line.astype(jnp.bfloat16).astype(jnp.float32)
        row = lax.broadcasted_iota(jnp.int32, (EXTRA, LANES), 0)
        packed = jnp.where(row == 0, line_high, jnp.where(row == 1, line - line_high, 0.0))
        part_out[body_rows:rows, :] = packed.astype(jnp.bfloat16)

    vmem = pl.BlockSpec(memory_space=pltpu.VMEM)
    return pl.pallas_call(
        body,
        out_shape=(
            jax.ShapeDtypeStruct((rows, LANES), jnp.bfloat16),
            jax.ShapeDtypeStruct((tokens, width), jnp.bfloat16),
            jax.ShapeDtypeStruct((1, cols), jnp.float32),
        ),
        in_specs=[pl.BlockSpec(memory_space=pltpu.SMEM)] + [vmem] * 9,
        out_specs=(vmem, vmem, vmem),
        name="tick",
        cost_estimate=pl.CostEstimate(flops=2 * tokens * width * cols, bytes_accessed=4 * width * tokens, transcendentals=0),
        compiler_params=pltpu.CompilerParams(vmem_limit_bytes=32 * 1024 * 1024),
    )


def on_device(layer_in, pre_act, weight, gain, cot_top):
    sections = lax.axis_size("section")
    parts = lax.axis_size("dp")
    section_idx = lax.axis_index("section")
    dp_idx = lax.axis_index("dp")
    inputs = layer_in[0]
    pre_acts = pre_act[0]
    micro, own_rows, width = inputs.shape
    tokens = own_rows * parts
    cols = width // parts
    pieces = cols // LANES
    share = sections // parts
    share_pieces = pieces // share
    body_rows = pieces * tokens
    local = micro * own_rows
    is_last = section_idx == sections - 1
    gain_cols = lax.dynamic_slice_in_dim(gain, dp_idx * cols, cols, axis=1)
    weight_t = weight[0].T

    inputs_f = inputs.astype(jnp.float32)
    mean_sq = jnp.mean(inputs_f * inputs_f, axis=-1).reshape(1, local)
    side = split3(mean_sq)[:, 0]
    side = jnp.pad(side, ((0, 13), (0, cols - local)))

    def by_target(value):
        return value.reshape(local, parts, cols).transpose(1, 0, 2)

    message = jnp.concatenate(
        [by_target(pre_acts), by_target(inputs), jnp.broadcast_to(side[None], (parts,) + side.shape)], axis=1
    )
    got = lax.all_to_all(message, "dp", split_axis=0, concat_axis=0, tiled=True)

    def as_pieces(value, count):
        value = value.reshape(parts, micro, own_rows, count, LANES)
        return value.transpose(1, 3, 0, 2, 4).reshape(micro, count * tokens, LANES)

    slope = slope_of(as_pieces(got[:, :local], pieces))
    slope = jnp.pad(slope, ((0, 0), (0, EXTRA), (0, 0)), constant_values=1.0)
    x_pieces = as_pieces(got[:, local : 2 * local], pieces)
    x_cols = got[:, local : 2 * local].reshape(parts, micro, own_rows, cols).transpose(1, 0, 2, 3)
    x_cols = x_cols.reshape(micro, tokens, cols)
    sq = jnp.sum(got[:, 2 * local : 2 * local + 3, :local].astype(jnp.float32), axis=1)
    sq = sq.reshape(parts, micro, own_rows).transpose(1, 0, 2).reshape(micro, tokens)
    row_scale = lax.rsqrt(sq + norm_eps)[..., None]
    scale_lanes = jnp.broadcast_to(row_scale, (micro, tokens, LANES))
    normed_cols = (x_cols.astype(jnp.float32) * row_scale * gain_cols).astype(jnp.bfloat16)

    x_upper = pass_down(x_pieces)
    inputs_upper = pass_down(inputs)
    upper_rows = (inputs_upper.astype(jnp.float32) * slope_of(pre_acts)).astype(jnp.bfloat16)
    upper_all = lax.all_gather(upper_rows, "dp", axis=0)

    top_all = as_pieces(spread(cot_top), share_pieces)
    top = []
    for i in range(share):
        pairs = [
            (d * sections + d * share + i, d * sections + sections - 1) for d in range(parts)
        ]
        top.append(lax.ppermute(top_all, ("dp", "section"), pairs))
    top = jnp.pad(jnp.concatenate(top, axis=1), ((0, 0), (0, EXTRA), (0, 0)))

    tick = tick_kernel(tokens, parts, width)

    def tick_step(tick_num, state):
        received, grad_store, gain_acc, bottom_store = state
        slot_pos = tick_num - (sections - 1 - section_idx)
        is_live = (slot_pos >= 0) & (slot_pos < micro)
        slot = jnp.clip(slot_pos, 0, micro - 1)
        pick = lambda buffer: lax.dynamic_index_in_dim(buffer, slot, 0, keepdims=False)
        part = jnp.where(is_last, pick(top), received)
        sent = (part.astype(jnp.float32) * pick(slope)).astype(jnp.bfloat16)
        gathered = spread(sent)
        upper = lax.dynamic_index_in_dim(upper_all, slot, 1, keepdims=False).reshape(tokens, width)
        part_new, pre_grad, gain_acc = tick(
            is_live.astype(jnp.int32).reshape(1),
            gathered,
            pltpu.with_memory_space_constraint(upper, pltpu.VMEM),
            pltpu.with_memory_space_constraint(weight_t, pltpu.VMEM),
            part,
            pick(x_upper),
            pick(x_pieces),
            pick(scale_lanes),
            gain_cols,
            gain_acc,
        )
        keep = jnp.where(slot_pos < micro, slot, micro)
        grad_store = lax.dynamic_update_index_in_dim(grad_store, pre_grad, keep, 0)
        bottom_store = lax.dynamic_update_index_in_dim(bottom_store, part_new, slot, 0)
        return (pass_down(part_new), grad_store, gain_acc, bottom_store)

    initial = (
        jnp.zeros((body_rows + EXTRA, LANES), jnp.bfloat16),
        jnp.zeros((micro + 1, tokens, width), jnp.bfloat16),
        jnp.zeros((1, cols), jnp.float32),
        jnp.zeros((micro, body_rows + EXTRA, LANES), jnp.bfloat16),
    )
    _, grad_store, gain_acc, bottom_store = lax.fori_loop(0, sections + micro - 1, tick_step, initial)

    own = jnp.sum(bottom_store[:, body_rows : body_rows + 2, :tokens].astype(jnp.float32), axis=1)
    own = jnp.sum(spread(own), axis=0)
    coef = jnp.tile(own, (1, pieces))[..., None]
    bottom = bottom_store[:, :body_rows].astype(jnp.float32) - coef * x_pieces.astype(jnp.float32)
    bottom = bottom.astype(jnp.bfloat16)
    part_rows = share_pieces * tokens
    mine = None
    for i in range(share):
        pairs = [(d * sections, d * sections + d * share + i) for d in range(parts)]
        moved = lax.ppermute(bottom[:, i * part_rows : (i + 1) * part_rows], ("dp", "section"), pairs)
        mine = moved if mine is None else jnp.where(section_idx % share == i, moved, mine)
    mine = mine.reshape(micro, share_pieces, parts, own_rows, LANES).transpose(2, 0, 3, 1, 4)
    mine = mine.reshape(parts, micro, own_rows, share_pieces * LANES)
    shares = lax.all_to_all(mine, "dp", split_axis=0, concat_axis=0, tiled=True)
    own_block = lax.dynamic_index_in_dim(shares, section_idx // share, 0, keepdims=False)

    weight_grad = jnp.einsum(
        "mki,mkj->ij", normed_cols, grad_store[:micro], preferred_element_type=jnp.float32
    ).astype(jnp.bfloat16)
    return (own_block, weight_grad[None], gain_acc)


def solution(mesh):
    return jax.shard_map(
        on_device,
        mesh=mesh,
        in_specs=(
            P("section", None, "dp", None),
            P("section", None, "dp", None),
            P("section", "dp", None),
            P("section", None),
            P(None, "dp", "section"),
        ),
        out_specs=(P(None, "dp", "section"), P("section", "dp", None), P("section", "dp")),
        check_vma=False,
    )
```

```python
import jax
import jax.numpy as jnp
from jax import lax
from jax.experimental import pallas as pl
from jax.experimental.pallas import tpu as pltpu
from jax.sharding import PartitionSpec as P

norm_eps = 1e-05
LANES = 128
EXTRA = 16
GROUP = 4
RING = 4
TURNS = (2, 1, 3)


def pass_down(value):
    count = lax.axis_size("section")
    return lax.ppermute(value, "section", [(source, source - 1) for source in range(1, count)])


def far_section():
    return lax.axis_size("section") // 2


def pass_near(value):
    count = lax.axis_size("section")
    pairs = [(source, source - 1) for source in range(1, count) if source != far_section()]
    return lax.ppermute(value, "section", pairs)


def pass_far(value):
    return lax.ppermute(value, "section", [(far_section(), far_section() - 1)])


def move(value, across, along):
    pairs = []
    for d in range(lax.axis_size("dp")):
        half, place = divmod(d, RING)
        pairs.append((d, (half ^ across) * RING + (place + along) % RING))
    return lax.ppermute(value, "dp", pairs)


def gather_blocks(value):
    other = move(value, 1, 0)
    own_ring = [move(value, 0, turn) for turn in TURNS]
    return [value, other] + own_ring + [move(other, 0, turn) for turn in TURNS]


def block_owners():
    half, place = lax.axis_index("dp") // RING, lax.axis_index("dp") % RING
    own_ring = [half * RING + (place + RING - turn) % RING for turn in TURNS]
    other_ring = [(1 - half) * RING + (place + RING - turn) % RING for turn in TURNS]
    return [half * RING + place, (1 - half) * RING + place] + own_ring + other_ring


def spread(value):
    count = lax.axis_size("dp")
    copies = jnp.broadcast_to(value[None], (count,) + value.shape)
    return lax.all_to_all(copies, "dp", split_axis=0, concat_axis=0, tiled=True)


def slope_of(pre_acts):
    pre_f = pre_acts.astype(jnp.float32)
    sigmoid_z = jax.nn.sigmoid(pre_f)
    return sigmoid_z * (1.0 + pre_f * (1.0 - sigmoid_z))


def split3(value):
    high = value.astype(jnp.bfloat16)
    rest = value - high.astype(jnp.float32)
    mid = rest.astype(jnp.bfloat16)
    low = (rest - mid.astype(jnp.float32)).astype(jnp.bfloat16)
    return jnp.stack([high, mid, low])


def unset(shape, dtype):
    return pl.pallas_call(
        lambda out: None,
        out_shape=jax.ShapeDtypeStruct(shape, dtype),
        out_specs=pl.BlockSpec(memory_space=pltpu.HBM),
        name="unset",
    )()


EARLY = 5


def as_columns(block, tokens, pieces):
    return jnp.concatenate([block[j * tokens : (j + 1) * tokens, :] for j in range(pieces)], axis=1)


def columns_of(info, i, cols):
    return pl.ds(pl.multiple_of(info[5 + i] * cols, LANES), cols)


def fetch_upper(info, sources, buffer, sem, start, cols=None, i=0):
    copies = []
    for source in sources:
        view = source.at[info[4]]
        if cols is not None:
            view = view.at[:, columns_of(info, i, cols)]
        copies.append(pltpu.make_async_copy(view, buffer, sem))
    if start:
        for at, copy in enumerate(copies):
            if len(copies) == 1:
                copy.start()
            else:
                pl.when(info[3] == at)(copy.start)
    return copies[0]


def products(info, blocks, first, weight_t, uppers, upper_buf, weight_buf, sems, total, tokens, cols):
    count = len(blocks)
    pieces = cols // LANES
    waits = []
    for i in range(count):
        upper = fetch_upper(info, uppers, upper_buf.at[i], sems.at[i], True, cols, first + i)
        rows = pl.ds(pl.multiple_of(info[5 + first + i] * cols, LANES), cols)
        weight = pltpu.make_async_copy(weight_t.at[rows, :], weight_buf.at[i], sems.at[count + i])
        weight.start()
        waits.append((upper, weight))
    for i in range(count):
        for copy in waits[i]:
            copy.wait()
        left = jnp.concatenate([as_columns(blocks[i], tokens, pieces), upper_buf[i]], axis=0)
        total = total + jnp.dot(left, weight_buf[i], preferred_element_type=jnp.float32)
    return total


def specs(smem, vmem, anywhere):
    return (
        [pl.BlockSpec(memory_space=pltpu.SMEM)] * smem
        + [pl.BlockSpec(memory_space=pltpu.VMEM)] * vmem
        + [pl.BlockSpec(memory_space=pltpu.HBM)] * anywhere
    )


LIMIT = pltpu.CompilerParams(vmem_limit_bytes=32 * 1024 * 1024)


def in_hbm(value):
    return pltpu.with_memory_space_constraint(value, pltpu.HBM)


def early_kernel(tokens, parts, width, upper_count):
    cols = width // parts

    def body(info, *refs):
        blocks, weight_t, uppers = refs[:EARLY], refs[EARLY], refs[EARLY + 1 : EARLY + 1 + upper_count]
        out, upper_buf, weight_buf, sems = refs[EARLY + 1 + upper_count :]
        total = jnp.zeros((2 * tokens, cols), jnp.float32)
        out[...] = products(info, blocks, 0, weight_t, uppers, upper_buf, weight_buf, sems, total, tokens, cols)

    return pl.pallas_call(
        body,
        out_shape=jax.ShapeDtypeStruct((2 * tokens, cols), jnp.float32),
        in_specs=specs(1, EARLY, 1 + upper_count),
        out_specs=pl.BlockSpec(memory_space=pltpu.VMEM),
        scratch_shapes=[
            pltpu.VMEM((EARLY, tokens, cols), jnp.bfloat16),
            pltpu.VMEM((EARLY, cols, cols), jnp.bfloat16),
            pltpu.SemaphoreType.DMA((2 * EARLY,)),
        ],
        name="early",
        cost_estimate=pl.CostEstimate(
            flops=4 * tokens * width * cols, bytes_accessed=2 * EARLY * cols * cols, transcendentals=0
        ),
        compiler_params=LIMIT,
    )


def tick_kernel(tokens, parts, width, upper_count):
    cols = width // parts
    pieces = cols // LANES
    body_rows = pieces * tokens
    rows = body_rows + EXTRA
    late = parts - EARLY
    across = (((1,), (1,)), ((), ()))
    down = (((0,), (0,)), ((), ()))

    def body(info, *refs):
        blocks = refs[:parts]
        early, part, gain, acc_in = refs[parts : parts + 4]
        weight_t, x_upper_all, x_all, scale_all, slope_all, top_all = refs[parts + 4 : parts + 10]
        uppers = refs[parts + 10 : parts + 10 + upper_count]
        part_out, acc_out, slope_out, top_out, coef_out = refs[parts + 10 + upper_count : parts + 15 + upper_count]
        upper_buf, weight_buf, x_upper, x_own, scale, sems, small_sems = refs[parts + 15 + upper_count :]
        slot, later = info[1], info[2]
        small = [
            pltpu.make_async_copy(x_upper_all.at[slot], x_upper, small_sems.at[0]),
            pltpu.make_async_copy(x_all.at[slot], x_own, small_sems.at[1]),
            pltpu.make_async_copy(scale_all.at[slot], scale, small_sems.at[2]),
            pltpu.make_async_copy(slope_all.at[later], slope_out, small_sems.at[3]),
            pltpu.make_async_copy(top_all.at[later], top_out, small_sems.at[4]),
        ]
        for copy in small:
            copy.start()
        sums = jnp.concatenate([block[body_rows:rows, :] for block in blocks], axis=0)
        coef = lax.dot_general(
            sums, jnp.ones((parts * EXTRA, LANES), jnp.bfloat16), down, preferred_element_type=jnp.float32
        )[:tokens]
        coef_out[...] = coef
        both = products(
            info, blocks[EARLY:], EARLY, weight_t, uppers, upper_buf, weight_buf, sems, early[...], tokens, cols
        )
        for copy in small[:3]:
            copy.wait()
        scale_v = scale[...]
        total = jnp.zeros((tokens, LANES), jnp.float32)
        for j in range(pieces):
            here = slice(j * tokens, (j + 1) * tokens)
            lanes = slice(j * LANES, (j + 1) * LANES)
            grad_j = both[:tokens, lanes] - coef * both[tokens:, lanes]
            x_j = x_own[here, :].astype(jnp.float32)
            scaled = gain[:, lanes] * grad_j
            incoming = part[here, :].astype(jnp.float32) - coef * x_upper[here, :].astype(jnp.float32)
            part_out[here, :] = (incoming + scale_v * scaled).astype(jnp.bfloat16)
            total = total + scaled * x_j
            gain_sum = jnp.sum(grad_j * x_j * scale_v, axis=0, keepdims=True)
            acc_out[:, lanes] = acc_in[:, lanes] + jnp.where(info[0] > 0, gain_sum, 0.0)
        total = total * (scale_v * scale_v * scale_v * (1.0 / width))
        if tokens < LANES:
            total = jnp.concatenate([total, jnp.zeros((LANES - tokens, LANES), jnp.float32)], axis=0)
        high = total.astype(jnp.bfloat16)
        low = (total - high.astype(jnp.float32)).astype(jnp.bfloat16)
        ones = jnp.ones((EXTRA, LANES), jnp.bfloat16)
        line = lax.dot_general(ones, high, across, preferred_element_type=jnp.float32)
        line = line + lax.dot_general(ones, low, across, preferred_element_type=jnp.float32)
        line_high = line.astype(jnp.bfloat16).astype(jnp.float32)
        row = lax.broadcasted_iota(jnp.int32, (EXTRA, LANES), 0)
        packed = jnp.where(row == 0, line_high, jnp.where(row == 1, line - line_high, 0.0))
        part_out[body_rows:rows, :] = packed.astype(jnp.bfloat16)
        for copy in small[3:]:
            copy.wait()

    return pl.pallas_call(
        body,
        out_shape=(
            jax.ShapeDtypeStruct((rows, LANES), jnp.bfloat16),
            jax.ShapeDtypeStruct((1, cols), jnp.float32),
            jax.ShapeDtypeStruct((rows, LANES), jnp.float32),
            jax.ShapeDtypeStruct((rows, LANES), jnp.bfloat16),
            jax.ShapeDtypeStruct((tokens, LANES), jnp.float32),
        ),
        in_specs=specs(1, parts + 4, 6 + upper_count),
        out_specs=(pl.BlockSpec(memory_space=pltpu.VMEM),) * 5,
        scratch_shapes=[
            pltpu.VMEM((late, tokens, cols), jnp.bfloat16),
            pltpu.VMEM((late, cols, cols), jnp.bfloat16),
            pltpu.VMEM((body_rows, LANES), jnp.bfloat16),
            pltpu.VMEM((body_rows, LANES), jnp.bfloat16),
            pltpu.VMEM((tokens, LANES), jnp.float32),
            pltpu.SemaphoreType.DMA((2 * late,)),
            pltpu.SemaphoreType.DMA((5,)),
        ],
        name="tick",
        cost_estimate=pl.CostEstimate(
            flops=4 * tokens * width * cols, bytes_accessed=2 * late * cols * cols, transcendentals=0
        ),
        compiler_params=LIMIT,
    )


def grads_kernel(tokens, parts, width, upper_count, slots):
    cols = width // parts
    pieces = cols // LANES

    def body(info, *refs):
        blocks, coef_ref = refs[:parts], refs[parts]
        uppers = refs[parts + 1 : parts + 1 + upper_count]
        _, store, out, upper, sem = refs[parts + 1 + upper_count :]
        copy = fetch_upper(info, uppers, upper, sem, True)
        coef = coef_ref[...]
        copy.wait()
        for i in range(parts):
            for j in range(pieces):
                at = pl.ds(pl.multiple_of(info[5 + i] * cols + j * LANES, LANES), LANES)
                piece = blocks[i][j * tokens : (j + 1) * tokens, :].astype(jnp.float32)
                out[:, at] = (piece - coef * upper[:, at].astype(jnp.float32)).astype(jnp.bfloat16)
        back = pltpu.make_async_copy(out, store.at[info[5 + parts]], sem)
        back.start()
        back.wait()

    return pl.pallas_call(
        body,
        out_shape=jax.ShapeDtypeStruct((slots, tokens, width), jnp.bfloat16),
        in_specs=specs(1, parts + 1, upper_count + 1),
        out_specs=pl.BlockSpec(memory_space=pltpu.HBM),
        input_output_aliases={parts + 2 + upper_count: 0},
        scratch_shapes=[
            pltpu.VMEM((tokens, width), jnp.bfloat16),
            pltpu.VMEM((tokens, width), jnp.bfloat16),
            pltpu.SemaphoreType.DMA,
        ],
        name="grads",
        cost_estimate=pl.CostEstimate(flops=2 * tokens * width, bytes_accessed=6 * tokens * width, transcendentals=0),
        compiler_params=LIMIT,
    )


def on_device(layer_in, pre_act, weight, gain, cot_top):
    sections = lax.axis_size("section")
    parts = lax.axis_size("dp")
    section_idx = lax.axis_index("section")
    dp_idx = lax.axis_index("dp")
    inputs = layer_in[0]
    pre_acts = pre_act[0]
    micro, own_rows, width = inputs.shape
    tokens = own_rows * parts
    cols = width // parts
    pieces = cols // LANES
    share = sections // parts
    share_pieces = pieces // share
    body_rows = pieces * tokens
    groups = micro // GROUP
    is_last = section_idx == sections - 1
    gain_cols = lax.dynamic_slice_in_dim(gain, dp_idx * cols, cols, axis=1)
    weight_rows = weight[0]
    weight_t = weight_rows.T

    def as_pieces(value, count, own):
        value = value.reshape(parts, -1, own, count, LANES)
        return value.transpose(1, 3, 0, 2, 4).reshape(-1, count * parts * own, LANES)

    def prepare(first, last, token):
        count = last - first
        local = count * own_rows
        x = inputs[first:last]
        x_f = x.astype(jnp.float32)
        side = split3(jnp.mean(x_f * x_f, axis=-1).reshape(1, local))[:, 0]
        side = jnp.pad(side, ((0, EXTRA - 3), (0, cols - local)))
        if token is not None:
            side = side + token
        ends = cot_top[first:last].reshape(local // share, cols)
        both = jnp.concatenate([side, ends], axis=0)
        message = jnp.concatenate(
            [
                pre_acts[first:last].reshape(local, parts, cols).transpose(1, 0, 2),
                x.reshape(local, parts, cols).transpose(1, 0, 2),
                jnp.broadcast_to(both[None], (parts,) + both.shape),
            ],
            axis=1,
        )
        got = lax.all_to_all(message, "dp", split_axis=0, concat_axis=0, tiled=True)
        slope = slope_of(as_pieces(got[:, :local], pieces, own_rows))
        slope = jnp.pad(slope, ((0, 0), (0, EXTRA), (0, 0)), constant_values=1.0)
        x_got = got[:, local : 2 * local]
        x_pieces = as_pieces(x_got, pieces, own_rows)
        sq = jnp.sum(got[:, 2 * local : 2 * local + 3, :local].astype(jnp.float32), axis=1)
        if token is None:
            sq = sq + weight_t[0, 0].astype(jnp.float32) * 0
        sq = sq.reshape(parts, count, own_rows).transpose(1, 0, 2).reshape(count, tokens)
        row_scale = lax.rsqrt(sq + norm_eps)[..., None]
        x_cols = x_got.reshape(parts, count, own_rows, cols).transpose(1, 0, 2, 3).reshape(count, tokens, cols)
        normed = (x_cols.astype(jnp.float32) * row_scale * gain_cols).astype(jnp.bfloat16)
        top_all = got[:, 2 * local + EXTRA :].reshape(parts, local, cols // share)
        top_all = as_pieces(top_all, share_pieces, own_rows)
        top = []
        for i in range(share):
            pairs = [(d * sections + d * share + i, d * sections + sections - 1) for d in range(parts)]
            top.append(lax.ppermute(top_all, ("dp", "section"), pairs))
        top = jnp.pad(jnp.concatenate(top, axis=1), ((0, 0), (0, EXTRA), (0, 0)))
        small = (
            pass_down(x_pieces),
            x_pieces,
            jnp.broadcast_to(row_scale, (count, tokens, LANES)),
            slope,
            top,
        )
        return small, normed, sq[0, 0].astype(jnp.bfloat16) * 0

    def upper_terms(first, token):
        here = slice(first, first + GROUP)
        upper = pass_down(inputs[here]).astype(jnp.float32) * slope_of(pre_acts[here])
        upper = upper.astype(jnp.bfloat16)
        if token is not None:
            upper = upper + token
        return lax.all_gather(upper, "dp", axis=1, tiled=True)

    owners = block_owners()

    after = (sections - 1 - section_idx) + (section_idx < far_section()).astype(jnp.int32)

    def slot_of(tick_num, count):
        return jnp.clip(tick_num - after, 0, count - 1)

    def run(first, last, small, uppers, state):
        sizes = (tokens, parts, width, len(uppers))
        early, tick = early_kernel(*sizes), tick_kernel(*sizes)
        grads = grads_kernel(*sizes, micro + 1)
        here = small[0].shape[0]
        ready = uppers[0].shape[0] * len(uppers)

        def tick_step(tick_num, state):
            near, far, newest, slope_here, top_here, grad_store, gain_acc, bottom_store = state
            far_next = pass_far(newest)
            slot_pos = tick_num - after
            is_live = (slot_pos >= 0) & (slot_pos < micro)
            slot = slot_of(tick_num, here)
            upper_slot = jnp.minimum(slot, ready - 1)
            received = jnp.where(section_idx == far_section() - 1, far, near)
            part = jnp.where(is_last, top_here, received)
            sent = (part.astype(jnp.float32) * slope_here).astype(jnp.bfloat16)
            group = uppers[0].shape[0]
            keep = jnp.where(slot_pos < micro, slot, micro)
            scalars = [is_live, slot, slot_of(tick_num + 1, here), upper_slot // group, upper_slot % group]
            info = jnp.stack([v.astype(jnp.int32) for v in scalars + owners + [keep]])
            blocks = gather_blocks(sent)
            weight_here = in_hbm(weight_t)
            uppers_here = [in_hbm(value) for value in uppers]
            small_here = [in_hbm(value) for value in small]
            early_sums = early(info, *blocks[:EARLY], weight_here, *uppers_here)
            newest, gain_acc, slope_here, top_here, coef = tick(
                info, *blocks, early_sums, part, gain_cols, gain_acc, weight_here, *small_here, *uppers_here
            )
            grad_store = grads(info, *blocks, coef, *uppers_here, in_hbm(grad_store))
            bottom_store = lax.dynamic_update_index_in_dim(bottom_store, newest, slot, 0)
            return (pass_near(newest), far_next, newest, slope_here, top_here, grad_store, gain_acc, bottom_store)

        return lax.fori_loop(first, last, tick_step, state)

    ticks = sections + micro
    small, normed, token = prepare(0, micro, None)
    uppers = [upper_terms(first, token if first else None) for first in range(0, micro, GROUP)]
    empty = jnp.zeros((body_rows + EXTRA, LANES), jnp.bfloat16)
    state = (
        empty,
        empty,
        empty,
        small[3][0],
        small[4][0],
        unset((micro + 1, tokens, width), jnp.bfloat16),
        jnp.zeros((1, cols), jnp.float32),
        unset((micro, body_rows + EXTRA, LANES), jnp.bfloat16),
    )
    state = run(0, 1, small, [weight_rows.reshape(-1, tokens, width)], state)
    state = run(1, GROUP, small, uppers[:1], state)
    for group in range(1, groups):
        last = ticks if group + 1 == groups else (group + 1) * GROUP
        state = run(group * GROUP, last, small, uppers[: group + 1], state)
    grad_store, gain_acc, bottom_store = state[5:]

    own = jnp.sum(bottom_store[:, body_rows : body_rows + 2, :tokens].astype(jnp.float32), axis=1)
    own = jnp.sum(spread(own), axis=0)
    coef = jnp.tile(own, (1, pieces))[..., None]
    bottom = bottom_store[:, :body_rows].astype(jnp.float32) - coef * small[1].astype(jnp.float32)
    bottom = bottom.astype(jnp.bfloat16)
    part_rows = share_pieces * tokens
    mine = None
    for i in range(share):
        pairs = [(d * sections, d * sections + d * share + i) for d in range(parts)]
        moved = lax.ppermute(bottom[:, i * part_rows : (i + 1) * part_rows], ("dp", "section"), pairs)
        mine = moved if mine is None else jnp.where(section_idx % share == i, moved, mine)
    weight_grad = jnp.einsum(
        "mki,mkj->ij", normed, grad_store[:micro], preferred_element_type=jnp.float32
    ).astype(jnp.bfloat16)
    mine = mine + weight_grad[0, 0] * 0
    mine = mine.reshape(micro, share_pieces, parts, own_rows, LANES).transpose(2, 0, 3, 1, 4)
    mine = mine.reshape(parts, micro, own_rows, share_pieces * LANES)
    shares = lax.all_to_all(mine, "dp", split_axis=0, concat_axis=0, tiled=True)
    own_block = lax.dynamic_index_in_dim(shares, section_idx // share, 0, keepdims=False)
    return (own_block, weight_grad[None], gain_acc)


def solution(mesh):
    return jax.shard_map(
        on_device,
        mesh=mesh,
        in_specs=(
            P("section", None, "dp", None),
            P("section", None, "dp", None),
            P("section", "dp", None),
            P("section", None),
            P(None, "dp", "section"),
        ),
        out_specs=(P(None, "dp", "section"), P("section", "dp", None), P("section", "dp")),
        check_vma=False,
    )
```

```python
import jax
import jax.numpy as jnp
from jax import lax
from jax.experimental import pallas as pl
from jax.experimental.pallas import tpu as pltpu
from jax.sharding import PartitionSpec as P

norm_eps = 1e-05
LANES = 128
EXTRA = 16
GROUP = 4
RING = 4
TURNS = (2, 1, 3)


def pass_down(value):
    count = lax.axis_size("section")
    return lax.ppermute(value, "section", [(source, source - 1) for source in range(1, count)])


def far_section():
    return lax.axis_size("section") // 2


def pass_near(value):
    count = lax.axis_size("section")
    pairs = [(source, source - 1) for source in range(1, count) if source != far_section()]
    return lax.ppermute(value, "section", pairs)


def pass_far(value):
    return lax.ppermute(value, "section", [(far_section(), far_section() - 1)])


def move(value, across, along):
    pairs = []
    for d in range(lax.axis_size("dp")):
        half, place = divmod(d, RING)
        pairs.append((d, (half ^ across) * RING + (place + along) % RING))
    return lax.ppermute(value, "dp", pairs)


def gather_blocks(value):
    other = move(value, 1, 0)
    own_ring = [move(value, 0, turn) for turn in TURNS]
    return [value, other] + own_ring + [move(other, 0, turn) for turn in TURNS]


def block_owners():
    half, place = lax.axis_index("dp") // RING, lax.axis_index("dp") % RING
    own_ring = [half * RING + (place + RING - turn) % RING for turn in TURNS]
    other_ring = [(1 - half) * RING + (place + RING - turn) % RING for turn in TURNS]
    return [half * RING + place, (1 - half) * RING + place] + own_ring + other_ring


def spread(value):
    count = lax.axis_size("dp")
    copies = jnp.broadcast_to(value[None], (count,) + value.shape)
    return lax.all_to_all(copies, "dp", split_axis=0, concat_axis=0, tiled=True)


def slope_of(pre_acts):
    pre_f = pre_acts.astype(jnp.float32)
    sigmoid_z = jax.nn.sigmoid(pre_f)
    return sigmoid_z * (1.0 + pre_f * (1.0 - sigmoid_z))


def split3(value):
    high = value.astype(jnp.bfloat16)
    rest = value - high.astype(jnp.float32)
    mid = rest.astype(jnp.bfloat16)
    low = (rest - mid.astype(jnp.float32)).astype(jnp.bfloat16)
    return jnp.stack([high, mid, low])


def unset(shape, dtype):
    return pl.pallas_call(
        lambda out: None,
        out_shape=jax.ShapeDtypeStruct(shape, dtype),
        out_specs=pl.BlockSpec(memory_space=pltpu.HBM),
        name="unset",
    )()


EARLY = 5


def as_columns(block, tokens, pieces):
    return jnp.concatenate([block[j * tokens : (j + 1) * tokens, :] for j in range(pieces)], axis=1)


def columns_of(info, i, cols):
    return pl.ds(pl.multiple_of(info[5 + i] * cols, LANES), cols)


def fetch_upper(info, sources, buffer, sem, start, cols=None, i=0):
    copies = []
    for source in sources:
        view = source.at[info[4]]
        if cols is not None:
            view = view.at[:, columns_of(info, i, cols)]
        copies.append(pltpu.make_async_copy(view, buffer, sem))
    if start:
        for at, copy in enumerate(copies):
            if len(copies) == 1:
                copy.start()
            else:
                pl.when(info[3] == at)(copy.start)
    return copies[0]


def products(info, blocks, first, weight_t, uppers, upper_buf, weight_buf, sems, total, tokens, cols):
    count = len(blocks)
    pieces = cols // LANES
    waits = []
    for i in range(count):
        upper = fetch_upper(info, uppers, upper_buf.at[i], sems.at[i], True, cols, first + i)
        rows = pl.ds(pl.multiple_of(info[5 + first + i] * cols, LANES), cols)
        weight = pltpu.make_async_copy(weight_t.at[rows, :], weight_buf.at[i], sems.at[count + i])
        weight.start()
        waits.append((upper, weight))
    for i in range(count):
        for copy in waits[i]:
            copy.wait()
        left = jnp.concatenate([as_columns(blocks[i], tokens, pieces), upper_buf[i]], axis=0)
        total = total + jnp.dot(left, weight_buf[i], preferred_element_type=jnp.float32)
    return total


def specs(smem, vmem, anywhere):
    return (
        [pl.BlockSpec(memory_space=pltpu.SMEM)] * smem
        + [pl.BlockSpec(memory_space=pltpu.VMEM)] * vmem
        + [pl.BlockSpec(memory_space=pltpu.HBM)] * anywhere
    )


LIMIT = pltpu.CompilerParams(vmem_limit_bytes=32 * 1024 * 1024)


def in_hbm(value):
    return pltpu.with_memory_space_constraint(value, pltpu.HBM)


def early_kernel(tokens, parts, width, upper_count):
    cols = width // parts

    def body(info, *refs):
        blocks, weight_t, uppers = refs[:EARLY], refs[EARLY], refs[EARLY + 1 : EARLY + 1 + upper_count]
        out, upper_buf, weight_buf, sems = refs[EARLY + 1 + upper_count :]
        total = jnp.zeros((2 * tokens, cols), jnp.float32)
        out[...] = products(info, blocks, 0, weight_t, uppers, upper_buf, weight_buf, sems, total, tokens, cols)

    return pl.pallas_call(
        body,
        out_shape=jax.ShapeDtypeStruct((2 * tokens, cols), jnp.float32),
        in_specs=specs(1, EARLY, 1 + upper_count),
        out_specs=pl.BlockSpec(memory_space=pltpu.VMEM),
        scratch_shapes=[
            pltpu.VMEM((EARLY, tokens, cols), jnp.bfloat16),
            pltpu.VMEM((EARLY, cols, cols), jnp.bfloat16),
            pltpu.SemaphoreType.DMA((2 * EARLY,)),
        ],
        name="early",
        cost_estimate=pl.CostEstimate(
            flops=4 * tokens * width * cols, bytes_accessed=2 * EARLY * cols * cols, transcendentals=0
        ),
        compiler_params=LIMIT,
    )


def tick_kernel(tokens, parts, width, upper_count):
    cols = width // parts
    pieces = cols // LANES
    body_rows = pieces * tokens
    rows = body_rows + EXTRA
    late = parts - EARLY
    across = (((1,), (1,)), ((), ()))
    down = (((0,), (0,)), ((), ()))

    def body(info, *refs):
        blocks = refs[:parts]
        early, part, gain, acc_in = refs[parts : parts + 4]
        weight_t, x_upper_all, x_all, scale_all, slope_all, top_all = refs[parts + 4 : parts + 10]
        uppers = refs[parts + 10 : parts + 10 + upper_count]
        part_out, acc_out, slope_out, top_out, coef_out = refs[parts + 10 + upper_count : parts + 15 + upper_count]
        upper_buf, weight_buf, x_upper, x_own, scale, sems, small_sems = refs[parts + 15 + upper_count :]
        slot, later = info[1], info[2]
        small = [
            pltpu.make_async_copy(x_upper_all.at[slot], x_upper, small_sems.at[0]),
            pltpu.make_async_copy(x_all.at[slot], x_own, small_sems.at[1]),
            pltpu.make_async_copy(scale_all.at[slot], scale, small_sems.at[2]),
            pltpu.make_async_copy(slope_all.at[later], slope_out, small_sems.at[3]),
            pltpu.make_async_copy(top_all.at[later], top_out, small_sems.at[4]),
        ]
        for copy in small:
            copy.start()
        sums = jnp.concatenate([block[body_rows:rows, :] for block in blocks], axis=0)
        coef = lax.dot_general(
            sums, jnp.ones((parts * EXTRA, LANES), jnp.bfloat16), down, preferred_element_type=jnp.float32
        )[:tokens]
        coef_out[...] = coef
        both = products(
            info, blocks[EARLY:], EARLY, weight_t, uppers, upper_buf, weight_buf, sems, early[...], tokens, cols
        )
        for copy in small[:3]:
            copy.wait()
        scale_v = scale[...]
        total = jnp.zeros((tokens, LANES), jnp.float32)
        for j in range(pieces):
            here = slice(j * tokens, (j + 1) * tokens)
            lanes = slice(j * LANES, (j + 1) * LANES)
            grad_j = both[:tokens, lanes] - coef * both[tokens:, lanes]
            x_j = x_own[here, :].astype(jnp.float32)
            scaled = gain[:, lanes] * grad_j
            incoming = part[here, :].astype(jnp.float32) - coef * x_upper[here, :].astype(jnp.float32)
            part_out[here, :] = (incoming + scale_v * scaled).astype(jnp.bfloat16)
            total = total + scaled * x_j
            gain_sum = jnp.sum(grad_j * x_j * scale_v, axis=0, keepdims=True)
            acc_out[:, lanes] = acc_in[:, lanes] + jnp.where(info[0] > 0, gain_sum, 0.0)
        total = total * (scale_v * scale_v * scale_v * (1.0 / width))
        if tokens < LANES:
            total = jnp.concatenate([total, jnp.zeros((LANES - tokens, LANES), jnp.float32)], axis=0)
        high = total.astype(jnp.bfloat16)
        low = (total - high.astype(jnp.float32)).astype(jnp.bfloat16)
        ones = jnp.ones((EXTRA, LANES), jnp.bfloat16)
        line = lax.dot_general(ones, high, across, preferred_element_type=jnp.float32)
        line = line + lax.dot_general(ones, low, across, preferred_element_type=jnp.float32)
        line_high = line.astype(jnp.bfloat16).astype(jnp.float32)
        row = lax.broadcasted_iota(jnp.int32, (EXTRA, LANES), 0)
        packed = jnp.where(row == 0, line_high, jnp.where(row == 1, line - line_high, 0.0))
        part_out[body_rows:rows, :] = packed.astype(jnp.bfloat16)
        for copy in small[3:]:
            copy.wait()

    return pl.pallas_call(
        body,
        out_shape=(
            jax.ShapeDtypeStruct((rows, LANES), jnp.bfloat16),
            jax.ShapeDtypeStruct((1, cols), jnp.float32),
            jax.ShapeDtypeStruct((rows, LANES), jnp.float32),
            jax.ShapeDtypeStruct((rows, LANES), jnp.bfloat16),
            jax.ShapeDtypeStruct((tokens, LANES), jnp.float32),
        ),
        in_specs=specs(1, parts + 4, 6 + upper_count),
        out_specs=(pl.BlockSpec(memory_space=pltpu.VMEM),) * 5,
        scratch_shapes=[
            pltpu.VMEM((late, tokens, cols), jnp.bfloat16),
            pltpu.VMEM((late, cols, cols), jnp.bfloat16),
            pltpu.VMEM((body_rows, LANES), jnp.bfloat16),
            pltpu.VMEM((body_rows, LANES), jnp.bfloat16),
            pltpu.VMEM((tokens, LANES), jnp.float32),
            pltpu.SemaphoreType.DMA((2 * late,)),
            pltpu.SemaphoreType.DMA((5,)),
        ],
        name="tick",
        cost_estimate=pl.CostEstimate(
            flops=4 * tokens * width * cols, bytes_accessed=2 * late * cols * cols, transcendentals=0
        ),
        compiler_params=LIMIT,
    )


def grads_kernel(tokens, parts, width, upper_count, slots):
    cols = width // parts
    pieces = cols // LANES

    def body(info, *refs):
        blocks, coef_ref = refs[:parts], refs[parts]
        uppers = refs[parts + 1 : parts + 1 + upper_count]
        newest, _, _, store, bottom, out, upper, sem, bottom_sem = refs[parts + 1 + upper_count :]
        copy = fetch_upper(info, uppers, upper, sem, True)
        keep_newest = pltpu.make_async_copy(newest, bottom.at[info[1]], bottom_sem)
        keep_newest.start()
        coef = coef_ref[...]
        copy.wait()
        for i in range(parts):
            for j in range(pieces):
                at = pl.ds(pl.multiple_of(info[5 + i] * cols + j * LANES, LANES), LANES)
                piece = blocks[i][j * tokens : (j + 1) * tokens, :].astype(jnp.float32)
                out[:, at] = (piece - coef * upper[:, at].astype(jnp.float32)).astype(jnp.bfloat16)
        back = pltpu.make_async_copy(out, store.at[info[5 + parts]], sem)
        back.start()
        back.wait()
        keep_newest.wait()

    return pl.pallas_call(
        body,
        out_shape=(
            jax.ShapeDtypeStruct((slots, tokens, width), jnp.bfloat16),
            jax.ShapeDtypeStruct((slots - 1, pieces * tokens + EXTRA, LANES), jnp.bfloat16),
        ),
        in_specs=specs(1, parts + 1, upper_count) + specs(0, 1, 2),
        out_specs=(pl.BlockSpec(memory_space=pltpu.HBM),) * 2,
        input_output_aliases={parts + 3 + upper_count: 0, parts + 4 + upper_count: 1},
        scratch_shapes=[
            pltpu.VMEM((tokens, width), jnp.bfloat16),
            pltpu.VMEM((tokens, width), jnp.bfloat16),
            pltpu.SemaphoreType.DMA,
            pltpu.SemaphoreType.DMA,
        ],
        name="grads",
        cost_estimate=pl.CostEstimate(flops=2 * tokens * width, bytes_accessed=6 * tokens * width, transcendentals=0),
        compiler_params=LIMIT,
    )


def on_device(layer_in, pre_act, weight, gain, cot_top):
    sections = lax.axis_size("section")
    parts = lax.axis_size("dp")
    section_idx = lax.axis_index("section")
    dp_idx = lax.axis_index("dp")
    inputs = layer_in[0]
    pre_acts = pre_act[0]
    micro, own_rows, width = inputs.shape
    tokens = own_rows * parts
    cols = width // parts
    pieces = cols // LANES
    share = sections // parts
    share_pieces = pieces // share
    body_rows = pieces * tokens
    groups = micro // GROUP
    is_last = section_idx == sections - 1
    gain_cols = lax.dynamic_slice_in_dim(gain, dp_idx * cols, cols, axis=1)
    weight_rows = weight[0]
    weight_t = weight_rows.T

    def as_pieces(value, count, own):
        value = value.reshape(parts, -1, own, count, LANES)
        return value.transpose(1, 3, 0, 2, 4).reshape(-1, count * parts * own, LANES)

    def prepare(first, last, token):
        count = last - first
        local = count * own_rows
        x = inputs[first:last]
        x_f = x.astype(jnp.float32)
        side = split3(jnp.mean(x_f * x_f, axis=-1).reshape(1, local))[:, 0]
        side = jnp.pad(side, ((0, EXTRA - 3), (0, cols - local)))
        if token is not None:
            side = side + token
        ends = cot_top[first:last].reshape(local // share, cols)
        both = jnp.concatenate([side, ends], axis=0)
        message = jnp.concatenate(
            [
                pre_acts[first:last].reshape(local, parts, cols).transpose(1, 0, 2),
                x.reshape(local, parts, cols).transpose(1, 0, 2),
                jnp.broadcast_to(both[None], (parts,) + both.shape),
            ],
            axis=1,
        )
        got = lax.all_to_all(message, "dp", split_axis=0, concat_axis=0, tiled=True)
        slope = slope_of(as_pieces(got[:, :local], pieces, own_rows))
        slope = jnp.pad(slope, ((0, 0), (0, EXTRA), (0, 0)), constant_values=1.0)
        x_got = got[:, local : 2 * local]
        x_pieces = as_pieces(x_got, pieces, own_rows)
        sq = jnp.sum(got[:, 2 * local : 2 * local + 3, :local].astype(jnp.float32), axis=1)
        if token is None:
            sq = sq + weight_t[0, 0].astype(jnp.float32) * 0
        sq = sq.reshape(parts, count, own_rows).transpose(1, 0, 2).reshape(count, tokens)
        row_scale = lax.rsqrt(sq + norm_eps)[..., None]
        x_cols = x_got.reshape(parts, count, own_rows, cols).transpose(1, 0, 2, 3).reshape(count, tokens, cols)
        normed = (x_cols.astype(jnp.float32) * row_scale * gain_cols).astype(jnp.bfloat16)
        top_all = got[:, 2 * local + EXTRA :].reshape(parts, local, cols // share)
        top_all = as_pieces(top_all, share_pieces, own_rows)
        top = []
        for i in range(share):
            pairs = [(d * sections + d * share + i, d * sections + sections - 1) for d in range(parts)]
            top.append(lax.ppermute(top_all, ("dp", "section"), pairs))
        top = jnp.pad(jnp.concatenate(top, axis=1), ((0, 0), (0, EXTRA), (0, 0)))
        small = (
            pass_down(x_pieces),
            x_pieces,
            lax.optimization_barrier(jnp.broadcast_to(row_scale, (count, tokens, LANES))),
            slope,
            top,
        )
        return small, normed, sq[0, 0].astype(jnp.bfloat16) * 0

    def upper_terms(first, token):
        here = slice(first, first + GROUP)
        upper = pass_down(inputs[here]).astype(jnp.float32) * slope_of(pre_acts[here])
        upper = upper.astype(jnp.bfloat16)
        if token is not None:
            upper = upper + token
        return lax.all_gather(upper, "dp", axis=1, tiled=True)

    owners = block_owners()

    after = (sections - 1 - section_idx) + (section_idx < far_section()).astype(jnp.int32)

    def slot_of(tick_num, count):
        return jnp.clip(tick_num - after, 0, count - 1)

    def run(first, last, small, uppers, state):
        sizes = (tokens, parts, width, len(uppers))
        early, tick = early_kernel(*sizes), tick_kernel(*sizes)
        grads = grads_kernel(*sizes, micro + 1)
        here = small[0].shape[0]
        ready = uppers[0].shape[0] * len(uppers)

        def tick_step(tick_num, state):
            near, far, newest, slope_here, top_here, grad_store, gain_acc, bottom_store = state
            far_next = pass_far(newest)
            slot_pos = tick_num - after
            is_live = (slot_pos >= 0) & (slot_pos < micro)
            slot = slot_of(tick_num, here)
            upper_slot = jnp.minimum(slot, ready - 1)
            received = jnp.where(section_idx == far_section() - 1, far, near)
            part = jnp.where(is_last, top_here, received)
            sent = (part.astype(jnp.float32) * slope_here).astype(jnp.bfloat16)
            group = uppers[0].shape[0]
            keep = jnp.where(slot_pos < micro, slot, micro)
            scalars = [is_live, slot, slot_of(tick_num + 1, here), upper_slot // group, upper_slot % group]
            info = jnp.stack([v.astype(jnp.int32) for v in scalars + owners + [keep]])
            blocks = gather_blocks(sent)
            weight_here = in_hbm(weight_t)
            uppers_here = [in_hbm(value) for value in uppers]
            small_here = [in_hbm(value) for value in small]
            early_sums = early(info, *blocks[:EARLY], weight_here, *uppers_here)
            newest, gain_acc, slope_here, top_here, coef = tick(
                info, *blocks, early_sums, part, gain_cols, gain_acc, weight_here, *small_here, *uppers_here
            )
            grad_store, bottom_store = grads(
                info, *blocks, coef, *uppers_here, newest, in_hbm(grad_store), in_hbm(bottom_store)
            )
            return (pass_near(newest), far_next, newest, slope_here, top_here, grad_store, gain_acc, bottom_store)

        return lax.fori_loop(first, last, tick_step, state)

    ticks = sections + micro
    small, normed, token = prepare(0, micro, None)
    uppers = [upper_terms(first, token if first else None) for first in range(0, micro, GROUP)]
    empty = jnp.zeros((body_rows + EXTRA, LANES), jnp.bfloat16)
    state = (
        empty,
        empty,
        empty,
        small[3][0],
        small[4][0],
        unset((micro + 1, tokens, width), jnp.bfloat16),
        jnp.zeros((1, cols), jnp.float32),
        unset((micro, body_rows + EXTRA, LANES), jnp.bfloat16),
    )
    state = run(0, 1, small, [weight_rows.reshape(-1, tokens, width)], state)
    state = run(1, GROUP, small, uppers[:1], state)
    for group in range(1, groups):
        last = ticks if group + 1 == groups else (group + 1) * GROUP
        state = run(group * GROUP, last, small, uppers[: group + 1], state)
    grad_store, gain_acc, bottom_store = state[5:]

    own = jnp.sum(bottom_store[:, body_rows : body_rows + 2, :tokens].astype(jnp.float32), axis=1)
    own = jnp.sum(spread(own), axis=0)
    coef = jnp.tile(own, (1, pieces))[..., None]
    bottom = bottom_store[:, :body_rows].astype(jnp.float32) - coef * small[1].astype(jnp.float32)
    bottom = bottom.astype(jnp.bfloat16)
    part_rows = share_pieces * tokens
    mine = None
    for i in range(share):
        pairs = [(d * sections, d * sections + d * share + i) for d in range(parts)]
        moved = lax.ppermute(bottom[:, i * part_rows : (i + 1) * part_rows], ("dp", "section"), pairs)
        mine = moved if mine is None else jnp.where(section_idx % share == i, moved, mine)
    weight_grad = jnp.einsum(
        "mki,mkj->ij", normed, grad_store[:micro], preferred_element_type=jnp.float32
    ).astype(jnp.bfloat16)
    mine = mine + weight_grad[0, 0] * 0
    mine = mine.reshape(micro, share_pieces, parts, own_rows, LANES).transpose(2, 0, 3, 1, 4)
    mine = mine.reshape(parts, micro, own_rows, share_pieces * LANES)
    shares = lax.all_to_all(mine, "dp", split_axis=0, concat_axis=0, tiled=True)
    own_block = lax.dynamic_index_in_dim(shares, section_idx // share, 0, keepdims=False)
    return (own_block, weight_grad[None], gain_acc)


def solution(mesh):
    return jax.shard_map(
        on_device,
        mesh=mesh,
        in_specs=(
            P("section", None, "dp", None),
            P("section", None, "dp", None),
            P("section", "dp", None),
            P("section", None),
            P(None, "dp", "section"),
        ),
        out_specs=(P(None, "dp", "section"), P("section", "dp", None), P("section", "dp")),
        check_vma=False,
    )
```
